32 devices in a mesh: ctx: 8 (over y, x, core), head: 4 (over z).
Axes of the slice: x: 2, y: 2, z: 4, core: 2. Of those that a mesh axis runs over, the one named last changes fastest.
Arguments:
- q_linear: bfloat16 [2048, 8192], P('ctx', 'head'), may hold values from -4 to 4
- k_linear: bfloat16 [2048, 8192], P('ctx', 'head'), may hold values from -4 to 4
- v_linear: bfloat16 [2048, 8192], P('ctx', 'head'), may hold values from -40 to 40
- log_decay: float32 [2048, 64], P('ctx', 'head'), may hold values from -1 to 0
- norm_gain: float32 [8192], P('head'), may hold values from 0.5 to 1.5
- q_soft: bfloat16 [2048, 8192], P('ctx', 'head'), may hold values from -6 to 6
- k_soft: bfloat16 [2048, 1024], P('ctx'), may hold values from -4 to 4
- v_soft: bfloat16 [2048, 1024], P('ctx'), may hold values from -4 to 4
Outputs:
- linear_out: bfloat16 [2048, 8192], P('ctx', 'head')
- soft_out: bfloat16 [2048, 8192], P('ctx', 'head')
The draws below stay inside these ranges and needn't reach their ends.
All inputs are finite; a program needn't handle non-finite values.
Results may differ from the reference program's by a relative error of at most 0.0075.
Values may be sent and summed in bfloat16 or wider, within the bound.
A program may use at most 64 MiB of HBM per device.

```python
import math
import jax
import jax.numpy as jnp
from jax import lax

QUERY_HEADS = 64
DH = 128
KV_HEADS = 8
BLOCK = 256
TOK_DEV = 256
SEQUENCE_TOKENS = 2048


def head_kinds(key):
    key_kind = jax.random.fold_in(key, 17)
    fast_share = 0.2
    middle_share = 0.3
    kind_draw = jax.random.uniform(key_kind, (QUERY_HEADS,), jnp.float32)
    is_fast = kind_draw < fast_share
    is_middle = jnp.logical_and(kind_draw >= fast_share, kind_draw < fast_share + middle_share)
    return (is_fast, is_middle)


def draw_v_linear(key, part):
    key_noise = jax.random.fold_in(jax.random.fold_in(key, 11), 0)
    key_row = jax.random.fold_in(jax.random.fold_in(key, 11), 1)
    key_loud = jax.random.fold_in(jax.random.fold_in(key, 11), 3)
    col_count = QUERY_HEADS * DH
    block_count = SEQUENCE_TOKENS // BLOCK
    is_fast, is_middle = head_kinds(key)
    head_factor = jnp.where(jnp.logical_or(is_fast, is_middle), 1.0, 0.02)
    head_factor = jnp.repeat(head_factor, DH)
    col_scale = 0.1 * jnp.power(10.0, jnp.arange(col_count, dtype=jnp.float32) / (col_count - 1))
    row_scale = jnp.power(10.0, jax.random.uniform(key_row, (SEQUENCE_TOKENS, 1), jnp.float32))
    loud = jax.random.randint(key_loud, (block_count,), 0, 4) == 0
    loud = jnp.logical_or(loud, jnp.arange(block_count) == 0)
    block_level = jnp.repeat(jnp.where(loud, 1.0, 0.01), BLOCK)[:, None]
    noise = jnp.clip(jax.random.normal(key_noise, (SEQUENCE_TOKENS, col_count), jnp.float32), -4.0, 4.0)
    return (noise * col_scale[None, :] * head_factor[None, :] * row_scale * block_level).astype(jnp.bfloat16)


def draw_log_decay(key, part):
    key_quick, key_middle, key_slow, key_block, key_location, key_penalty = jax.random.split(jax.random.fold_in(key, 5), 6)
    is_fast, is_middle = head_kinds(key)
    quick_rate = jax.random.uniform(key_quick, (QUERY_HEADS,), jnp.float32, minval=1.0 / 50, maxval=1.0 / 30)
    middle_rate = jax.random.uniform(key_middle, (QUERY_HEADS,), jnp.float32, minval=1.2, maxval=1.5) / BLOCK
    slow_rate = jax.random.uniform(key_slow, (QUERY_HEADS,), jnp.float32, minval=0.1, maxval=0.4) / SEQUENCE_TOKENS
    base_rate = jnp.where(is_fast, quick_rate, jnp.where(is_middle, middle_rate, slow_rate))
    block_count = SEQUENCE_TOKENS // TOK_DEV
    block_factor = jnp.exp(jax.random.uniform(key_block, (block_count, 1, QUERY_HEADS), jnp.float32, minval=0.0, maxval=math.log(2.5)))
    block_factor = jnp.broadcast_to(block_factor, (block_count, TOK_DEV, QUERY_HEADS)).reshape(SEQUENCE_TOKENS, QUERY_HEADS)
    baseline_logarithm = -base_rate[None, :] * block_factor
    spike_row_picks = jax.random.randint(key_location, (3,), 0, SEQUENCE_TOKENS)
    spike_penalty = jax.random.uniform(key_penalty, (3, QUERY_HEADS), jnp.float32, minval=0.2, maxval=0.35)
    row_identifiers = jnp.arange(SEQUENCE_TOKENS)[:, None]
    spike_logarithm = jnp.zeros((SEQUENCE_TOKENS, QUERY_HEADS), jnp.float32)
    for total_number in range(3):
        spike_logarithm = spike_logarithm + jnp.where(row_identifiers == spike_row_picks[total_number], jnp.log(1.0 - spike_penalty[total_number])[None, :], 0.0)
    return (baseline_logarithm + spike_logarithm).astype(jnp.float32)


def soft_pair(key):
    key_query = jax.random.fold_in(jax.random.fold_in(key, 3), 0)
    key_keys = jax.random.fold_in(jax.random.fold_in(key, 3), 1)
    key_places = jax.random.fold_in(jax.random.fold_in(key, 3), 4)
    key_signs = jax.random.fold_in(jax.random.fold_in(key, 3), 5)
    col_count = QUERY_HEADS * DH
    key_width = KV_HEADS * DH
    queries = jnp.clip(jax.random.normal(key_query, (SEQUENCE_TOKENS, col_count), jnp.float32), -4.0, 4.0)
    key_rows = jnp.clip(jax.random.normal(key_keys, (SEQUENCE_TOKENS, key_width), jnp.float32), -4.0, 4.0)
    row_identifiers = jnp.arange(SEQUENCE_TOKENS)[:, None]
    loud_places = jax.random.randint(key_places, (16,), 0, SEQUENCE_TOKENS)
    loud_signs = jnp.where(jax.random.normal(key_signs, (16, col_count), jnp.float32) >= 0.0, 6.0, -6.0)
    for loud_number in range(16):
        queries = jnp.where(row_identifiers == loud_places[loud_number], loud_signs[loud_number][None, :], queries)
    return (queries, key_rows)


def draw_q_soft(key, part):
    return soft_pair(key)[0].astype(jnp.bfloat16)


def draw_k_soft(key, part):
    return soft_pair(key)[1].astype(jnp.bfloat16)


def levels(key, dims, cuts, least, largest):
    def one(position, shards_of):
        heights = jax.random.uniform(jax.random.fold_in(jax.random.fold_in(key, 6), position), (shards_of,), jnp.float32, least / len(cuts), largest / len(cuts))
        return jnp.repeat(jnp.exp(heights), dims[position] // shards_of).reshape((-1,) + (1,) * (len(dims) - position - 1))

    loudness = one(*cuts[0])
    for cut in cuts[1:]:
        loudness = loudness * one(*cut)
    return loudness


def normal_values(key, shape, spread, most, shards=(), held_as=jnp.bfloat16):
    array = spread * jax.random.normal(key, shape, jnp.float32)
    if shards:
        array = array * levels(key, shape, shards, -0.22, 0.18)
    return jnp.clip(array, -most, most).astype(held_as)


def setup_inputs(seed: int = 0) -> dict:
    streams_of = jax.random.split(jax.random.key(seed), 9)
    return {
        "q_linear": normal_values(streams_of[0], (SEQUENCE_TOKENS, QUERY_HEADS * DH), 1.0, 4.0, ((0, 8), (1, 4))),
        "k_linear": normal_values(streams_of[1], (SEQUENCE_TOKENS, QUERY_HEADS * DH), 1.0, 4.0, ((0, 8), (1, 4))),
        "v_linear": draw_v_linear(jax.random.fold_in(streams_of[8], 71), 0),
        "log_decay": draw_log_decay(jax.random.fold_in(streams_of[8], 71), 0),
        "norm_gain": jnp.clip(1.0 + 0.1 * jax.random.normal(streams_of[4], (QUERY_HEADS * DH,), jnp.float32), 0.5, 1.5),
        "q_soft": draw_q_soft(jax.random.fold_in(streams_of[8], 71), 0),
        "k_soft": draw_k_soft(jax.random.fold_in(streams_of[8], 71), 0),
        "v_soft": normal_values(streams_of[7], (SEQUENCE_TOKENS, KV_HEADS * DH), 1.0, 4.0, ((0, 8),)),
    }


EPSILON = 1e-06
NEGATIVE = -1e+30

def lightning_block(running, inputs):
    queries, key_rows, value_rows, log_gates = inputs
    row_count = queries.shape[0]
    cumulative = jnp.cumsum(log_gates, axis=0)
    final_log = cumulative[-1]
    positions = jnp.arange(row_count, dtype=jnp.int32)
    causal = positions[None, :] <= positions[:, None]
    cum_heads = cumulative.T
    log_gap = jnp.where(causal[None], cum_heads[:, :, None] - cum_heads[:, None, :], NEGATIVE)
    scores = jnp.einsum('thd,shd->hts', queries.astype(jnp.float32), key_rows.astype(jnp.float32))
    weights = (scores * jnp.exp(log_gap)).astype(jnp.bfloat16)
    weights = lax.optimization_barrier(weights)
    intra_part = jnp.einsum('hts,she->the', weights.astype(jnp.float32), value_rows.astype(jnp.float32))
    lifted = queries.astype(jnp.float32) * jnp.exp(cumulative)[:, :, None]
    carried = jnp.einsum('thd,hde->the', lifted, running, precision=lax.Precision.HIGHEST)
    scaled = (key_rows.astype(jnp.float32) * jnp.exp(final_log[None, :] - cumulative)[:, :, None]).astype(jnp.bfloat16)
    scaled = lax.optimization_barrier(scaled)
    block_state = jnp.einsum('shd,she->hde', scaled.astype(jnp.float32), value_rows.astype(jnp.float32))
    running = jnp.exp(final_log)[:, None, None] * running + block_state
    return (running, intra_part + carried)

def soft_update(running, queries, query_pos, key_rows, value_rows, key_pos):
    row_max, row_total, weighted = running
    scores = jnp.einsum('thd,shd->hts', queries.astype(jnp.float32), key_rows.astype(jnp.float32)) * DH ** (-0.5)
    allowed = key_pos[None, :] <= query_pos[:, None]
    scores = jnp.where(allowed[None], scores, NEGATIVE)
    new_max = jnp.maximum(row_max, lax.optimization_barrier(jnp.max(scores, axis=2)))
    probabilities = jnp.where(allowed[None], jnp.exp(scores - new_max[:, :, None]), 0.0)
    rescale = jnp.exp(row_max - new_max)
    row_total = row_total * rescale + lax.optimization_barrier(jnp.sum(probabilities, axis=2))
    rounded = lax.optimization_barrier(probabilities.astype(jnp.bfloat16))
    weighted = weighted * rescale[:, :, None] + jnp.einsum('hts,she->hte', rounded.astype(jnp.float32), value_rows.astype(jnp.float32))
    return (new_max, row_total, weighted)

def reference(q_linear, k_linear, v_linear, log_decay, norm_gain, q_soft, k_soft, v_soft):
    block_count = SEQUENCE_TOKENS // BLOCK
    lin_shape = (block_count, BLOCK, QUERY_HEADS, DH)
    sequences = (q_linear.reshape(lin_shape), k_linear.reshape(lin_shape), v_linear.reshape(lin_shape), log_decay.reshape(block_count, BLOCK, QUERY_HEADS))
    initial = jnp.zeros((QUERY_HEADS, DH, DH), jnp.float32)
    _, mixed = lax.scan(lightning_block, initial, sequences)
    mixed = mixed.reshape(SEQUENCE_TOKENS, QUERY_HEADS * DH)
    power = lax.optimization_barrier(jnp.mean(mixed * mixed, axis=1, keepdims=True))
    linear_out = (mixed * lax.rsqrt(power + EPSILON) * norm_gain.astype(jnp.float32)[None, :]).astype(jnp.bfloat16)
    query_count = SEQUENCE_TOKENS // TOK_DEV
    group_size = QUERY_HEADS // KV_HEADS
    query_blocks = q_soft.reshape(query_count, TOK_DEV, QUERY_HEADS, DH)
    key_blocks = k_soft.reshape(query_count, TOK_DEV, KV_HEADS, DH)
    value_blocks = v_soft.reshape(query_count, TOK_DEV, KV_HEADS, DH)
    positions = jnp.arange(TOK_DEV, dtype=jnp.int32)
    block_ids = jnp.arange(query_count, dtype=jnp.int32)

    def one_query(inputs):
        queries, block_index = inputs
        query_pos = block_index * TOK_DEV + positions
        initial_soft = (jnp.full((QUERY_HEADS, TOK_DEV), NEGATIVE, jnp.float32), jnp.zeros((QUERY_HEADS, TOK_DEV), jnp.float32), jnp.zeros((QUERY_HEADS, TOK_DEV, DH), jnp.float32))

        def over_keys(running, other):
            key_rows, value_rows, key_index = other
            wide_keys = jnp.repeat(key_rows, group_size, axis=1)
            wide_values = jnp.repeat(value_rows, group_size, axis=1)
            updated = lax.cond(key_index <= block_index, lambda state: soft_update(state, queries, query_pos, wide_keys, wide_values, key_index * TOK_DEV + positions), lambda state: state, running)
            return (updated, None)
        (row_max, row_total, weighted), _ = lax.scan(over_keys, initial_soft, (key_blocks, value_blocks, block_ids))
        return jnp.transpose(weighted / row_total[:, :, None], (1, 0, 2))
    attended = lax.map(one_query, (query_blocks, block_ids))
    soft_out = attended.reshape(SEQUENCE_TOKENS, QUERY_HEADS * DH).astype(jnp.bfloat16)
    return (linear_out, soft_out)
```

```python
import functools

import jax
import jax.numpy as jnp
from jax import lax
from jax.experimental import pallas as pl
from jax.experimental.pallas import tpu as pltpu
from jax.sharding import PartitionSpec as P

QUERY_HEADS = 64
DH = 128
KV_HEADS = 8
EPSILON = 1e-06
NEGATIVE = -1e30
LOG2E = 1.4426950408889634
MESH = pl.DeviceIdType.MESH
F32 = jnp.float32
BF16 = jnp.bfloat16
HIGHEST = lax.Precision.HIGHEST


def mm(a, b, ca, cb, precision=None):
    return lax.dot_general(
        a, b, (((ca,), (cb,)), ((), ())), preferred_element_type=F32, precision=precision
    )


def cols(index):
    return pl.ds(pl.multiple_of(index * DH, DH), DH)


def kernel(
    n, zn, heads, kvc, ch,
    ld_ref, gain_ref, ql_hbm, kl_hbm, vl_hbm, qs_hbm, ks_hbm, vs_hbm,
    lin_hbm, soft_hbm,
    ql, kl, vl, qs, kv, lin, soft, cumc, cumr, state, mixed, ein, eout, mx, tot, acc, pw,
    in_sem, own_sem, out_sem, kv_recv, dir_send, sib_send, rel_send, ch_send, ch_recv, pw_send, pw_recv,
):
    c = lax.axis_index("ctx")
    z = lax.axis_index("head")
    rows = ql.shape[0]
    chips = n // 2
    chip, core = c // 2, c % 2
    sib = chip * 2 + 1 - core
    group = heads // kvc
    chunks = heads // ch

    start = pl.multiple_of((z * heads // (QUERY_HEADS // KV_HEADS)) * DH, DH)
    own = [
        pltpu.make_async_copy(src.at[:, pl.ds(start, kvc * DH)], kv.at[c, i], own_sem.at[i])
        for i, src in enumerate((ks_hbm, vs_hbm))
    ]
    loads = [
        pltpu.make_async_copy(src, dst, in_sem.at[i])
        for i, (src, dst) in enumerate(((kl_hbm, kl), (vl_hbm, vl), (ql_hbm, ql), (qs_hbm, qs)))
    ]
    for copy in own + loads:
        copy.start()

    barrier = pltpu.get_barrier_semaphore()
    for d in range(1, n):
        pl.semaphore_signal(barrier, inc=1, device_id={"ctx": lax.rem(c + d, n)}, device_id_type=MESH)
    for d in range(1, zn):
        pl.semaphore_signal(barrier, inc=1, device_id={"head": lax.rem(z + d, zn)}, device_id_type=MESH)
    pl.semaphore_wait(barrier, n - 1 + zn - 1)

    def kv_copy(block, i, send, target):
        return pltpu.make_async_remote_copy(
            src_ref=kv.at[block, i], dst_ref=kv.at[block, i],
            send_sem=send, recv_sem=kv_recv.at[block, i],
            device_id={"ctx": target}, device_id_type=MESH,
        )

    def direct(i, to):
        return kv_copy(c, i, dir_send.at[to, i], to * 2 + core)

    def sibling(i):
        return kv_copy(c, i, sib_send.at[i], sib)

    def relayed(i, source):
        return kv_copy(source * 2 + core, i, rel_send.at[source, i], sib)

    def arrived(block, i):
        kv_copy(block, i, sib_send.at[i], sib).wait_recv()

    for copy in own:
        copy.wait()

    @pl.when(core == 0)
    def _():
        for i in range(2):
            sibling(i).start()

    def send_direct(to, _):
        for i in range(2):
            direct(i, to).start()
        return 0

    lax.fori_loop(chip + 1, chips, send_direct, 0)

    row_id = lax.broadcasted_iota(jnp.int32, (rows, rows), 0)
    col_id = lax.broadcasted_iota(jnp.int32, (rows, rows), 1)
    tri = jnp.where(col_id <= row_id, 1.0, 0.0).astype(F32)
    ld = ld_ref[...]
    cum = mm(tri, ld, 1, 0, HIGHEST)
    cumr[...] = cum.T
    for h in range(heads):
        cumc[h] = jnp.broadcast_to(cum[:, h : h + 1], (rows, DH))
    for copy in loads[:2]:
        copy.wait()

    def states(h):
        cc = cumc[h]
        last = cc[rows - 1 : rows, :]
        decayed = (kl[:, cols(h)].astype(F32) * jnp.exp(last - cc)).astype(BF16)
        state[h] = mm(decayed, vl[:, cols(h)], 0, 0)

    def over_heads(body, count, unroll):
        unroll = min(unroll, count)

        def step(j, _):
            for u in range(unroll):
                body(j * unroll + u)
            return 0

        lax.fori_loop(0, count // unroll, step, 0)

    over_heads(states, heads, 4)
    for copy in loads[2:]:
        copy.wait()

    def intra(h):
        raw = mm(ql[:, cols(h)], kl[:, cols(h)], 1, 1)
        cc = cumc[h]
        gap = jnp.concatenate([cc] * (rows // DH), axis=1) - cumr[pl.ds(h, 1), :]
        r = lax.broadcasted_iota(jnp.int32, (rows, rows), 0)
        s = lax.broadcasted_iota(jnp.int32, (rows, rows), 1)
        w = (raw * jnp.exp(jnp.where(s <= r, gap, NEGATIVE))).astype(BF16)
        mixed[h] = mm(w, vl[:, cols(h)], 1, 0)

    def chain_copy(j):
        return pltpu.make_async_remote_copy(
            src_ref=eout.at[pl.ds(j * ch, ch)], dst_ref=ein.at[pl.ds(j * ch, ch)],
            send_sem=ch_send.at[j], recv_sem=ch_recv.at[j],
            device_id={"ctx": jnp.minimum(c + 1, n - 1)}, device_id_type=MESH,
        )

    def first_chain():
        def step(j, _):
            part = pl.ds(j * ch, ch)
            eout[part] = state[part].astype(BF16)
            chain_copy(j).start()
            return 0

        lax.fori_loop(0, chunks, step, 0)

    def chain():
        def step(j, _):
            chain_copy(j).wait_recv()

            @pl.when(c < n - 1)
            def _():
                for u in range(ch):
                    h = j * ch + u
                    fade = jnp.exp(cumc[h, rows - 1 : rows, :])
                    eout[h] = (fade * ein[h].astype(F32) + state[h]).astype(BF16)
                chain_copy(j).start()

            for u in range(ch):
                h = j * ch + u
                carried = mm(ql[:, cols(h)], ein[h], 1, 0)
                mixed[h] = mixed[h] + carried * jnp.exp(cumc[h])
            return 0

        lax.fori_loop(0, chunks, step, 0)

    def power_copy(d):
        return pltpu.make_async_remote_copy(
            src_ref=pw.at[0], dst_ref=pw.at[zn - d],
            send_sem=pw_send.at[d], recv_sem=pw_recv.at[zn - d],
            device_id={"head": lax.rem(z + d, zn)}, device_id_type=MESH,
        )

    def power():
        def step(h, total):
            m = mixed[h]
            return total + m * m

        part = lax.fori_loop(0, heads, step, jnp.zeros((rows, DH), F32))
        pw[0] = mm(jnp.ones((8, DH), F32), part, 1, 1, HIGHEST)
        for d in range(1, zn):
            power_copy(d).start()

    scale = DH ** (-0.5) * LOG2E

    def group_dot(h, keys):
        return mm(qs[:, cols(h)], keys, 1, 1) * scale

    def soft_own():
        for g in range(kvc):
            keys = kv[c, 0, :, g * DH : (g + 1) * DH]
            values = kv[c, 1, :, g * DH : (g + 1) * DH]

            def one(u):
                h = g * group + u
                s = group_dot(h, keys)
                r = lax.broadcasted_iota(jnp.int32, (rows, rows), 0)
                t = lax.broadcasted_iota(jnp.int32, (rows, rows), 1)
                s = jnp.where(t <= r, s, NEGATIVE)
                top = jnp.max(s, axis=1, keepdims=True)
                p = jnp.exp2(s - top)
                mx[h] = jnp.broadcast_to(top, (rows, DH))
                tot[h] = sum(p[:, i : i + DH] for i in range(0, rows, DH))
                acc[h] = mm(p.astype(BF16), values, 1, 0)

            over_heads(one, group, 4)

    def soft_full(first, count):
        for g in range(kvc):
            part = slice(g * DH, (g + 1) * DH)
            keys = kv[pl.ds(first, count), 0, :, part].reshape(count * rows, DH)
            values = kv[pl.ds(first, count), 1, :, part].reshape(count * rows, DH)

            def one(u):
                h = g * group + u
                s = group_dot(h, keys)
                before = mx[h]
                top = jnp.maximum(before, jnp.max(s, axis=1, keepdims=True))
                fade = jnp.exp2(before - top)
                p = [jnp.exp2(s[:, i : i + DH] - top) for i in range(0, count * rows, DH)]
                mx[h] = top
                tot[h] = tot[h] * fade + sum(p)
                packed = jnp.concatenate([x.astype(BF16) for x in p], axis=1)
                acc[h] = acc[h] * fade + mm(packed, values, 1, 0)

            over_heads(one, group, 4)

    def relay(source):
        for i in range(2):
            arrived(source * 2 + core, i)
            relayed(i, source).start()

    def pair(source):
        for i in range(2):
            arrived(source * 2 + 1 - core, i)
        soft_full(source * 2, 2)

    @pl.when(c == 0)
    def _():
        first_chain()

    over_heads(intra, heads, 2)

    @pl.when(chip > 0)
    def _():
        relay(chip - 1)

    @pl.when(c == 0)
    def _():
        power()

    @pl.when(c == 1)
    def _():
        chain()
        power()

    soft_own()

    @pl.when(core == 1)
    def _():
        for i in range(2):
            arrived(c - 1, i)
        soft_full(c - 1, 1)

    @pl.when(chip > 0)
    def _():
        def step(k, _):
            source = chip - 1 - k

            @pl.when(source == 0)
            def _():
                chain()
                power()

            @pl.when(source > 0)
            def _():
                relay(source - 1)

            pair(source)
            return 0

        lax.fori_loop(0, chip, step, 0)

    def soft_end(h):
        total = jnp.sum(tot[h], axis=1, keepdims=True)
        soft[:, cols(h)] = (acc[h] / total).astype(BF16)

    over_heads(soft_end, heads, 2)
    soft_out = pltpu.make_async_copy(soft, soft_hbm, out_sem.at[0])
    soft_out.start()

    for d in range(1, zn):
        power_copy(d).wait_recv()
    squares = pw[0]
    for d in range(1, zn):
        squares = squares + pw[d]
    mean = mm(squares, jnp.full((8, DH), 0.125, F32), 0, 0, HIGHEST) / (QUERY_HEADS * DH)
    norm = lax.rsqrt(mean + EPSILON)

    def lin_end(h):
        lin[:, cols(h)] = (mixed[h] * norm * gain_ref[pl.ds(h, 1), :]).astype(BF16)

    over_heads(lin_end, heads, 2)
    lin_out = pltpu.make_async_copy(lin, lin_hbm, out_sem.at[1])
    lin_out.start()

    for d in range(1, zn):
        power_copy(d).wait_send()

    @pl.when(c < n - 1)
    def _():
        lax.fori_loop(0, chunks, lambda j, _: (chain_copy(j).wait_send(), 0)[1], 0)

    @pl.when(core == 0)
    def _():
        for i in range(2):
            sibling(i).wait_send()

    def sent_direct(to, _):
        for i in range(2):
            direct(i, to).wait_send()
        return 0

    lax.fori_loop(chip + 1, chips, sent_direct, 0)

    def sent_relay(source, _):
        for i in range(2):
            relayed(i, source).wait_send()
        return 0

    lax.fori_loop(0, chip, sent_relay, 0)
    soft_out.wait()
    lin_out.wait()


def local(n, zn, q_linear, k_linear, v_linear, log_decay, norm_gain, q_soft, k_soft, v_soft):
    rows, width = q_linear.shape
    heads = width // DH
    kvc = max(1, heads // (QUERY_HEADS // KV_HEADS))
    ch = 2
    anywhere = pl.BlockSpec(memory_space=pl.ANY)
    whole = pl.BlockSpec(memory_space=pltpu.VMEM)
    dma = pltpu.SemaphoreType.DMA
    chips = n // 2
    chunks = heads // ch
    out = jax.ShapeDtypeStruct((rows, width), BF16)
    wide = pltpu.VMEM((rows, width), BF16)
    per_head = pltpu.VMEM((heads, rows, DH), F32)
    return pl.pallas_call(
        functools.partial(kernel, n, zn, heads, kvc, ch),
        out_shape=(out, out),
        in_specs=[whole, whole] + [anywhere] * 6,
        out_specs=(anywhere, anywhere),
        scratch_shapes=[
            wide, wide, wide, wide,
            pltpu.VMEM((n, 2, rows, kvc * DH), BF16),
            wide, wide,
            per_head,
            pltpu.VMEM((heads, rows), F32),
            pltpu.VMEM((heads, DH, DH), F32),
            per_head,
            pltpu.VMEM((heads, DH, DH), BF16),
            pltpu.VMEM((heads, DH, DH), BF16),
            per_head, per_head, per_head,
            pltpu.VMEM((zn, 8, rows), F32),
            dma((4,)), dma((2,)), dma((2,)),
            dma((n, 2)), dma((chips, 2)), dma((2,)), dma((chips, 2)),
            dma((chunks,)), dma((chunks,)), dma((zn,)), dma((zn,)),
        ],
        compiler_params=pltpu.CompilerParams(
            collective_id=0, has_side_effects=True, vmem_limit_bytes=56 * 2**20
        ),
    )(log_decay, norm_gain.reshape(heads, DH), q_linear, k_linear, v_linear, q_soft, k_soft, v_soft)


def solution(mesh):
    n, zn = mesh.shape["ctx"], mesh.shape["head"]
    return jax.shard_map(
        functools.partial(local, n, zn),
        mesh=mesh,
        in_specs=(
            P("ctx", "head"), P("ctx", "head"), P("ctx", "head"), P("ctx", "head"),
            P("head"), P("ctx", "head"), P("ctx", None), P("ctx", None),
        ),
        out_specs=(P("ctx", "head"), P("ctx", "head")),
        check_vma=False,
    )
```

```python
import functools

import jax
import jax.numpy as jnp
from jax import lax
from jax.experimental import pallas as pl
from jax.experimental.pallas import tpu as pltpu
from jax.sharding import PartitionSpec as P

QUERY_HEADS = 64
DH = 128
KV_HEADS = 8
EPSILON = 1e-06
NEGATIVE = -1e30
OWN_HEADS = 8
FULL_HEADS = 8
LOG2E = 1.4426950408889634
MESH = pl.DeviceIdType.MESH
F32 = jnp.float32
BF16 = jnp.bfloat16
HIGHEST = lax.Precision.HIGHEST


def mm(a, b, ca, cb, precision=None):
    return lax.dot_general(
        a, b, (((ca,), (cb,)), ((), ())), preferred_element_type=F32, precision=precision
    )


def cols(index):
    return pl.ds(pl.multiple_of(index * DH, DH), DH)


def kernel(
    n, zn, heads, kvc, ch,
    ld_ref, gain_ref, ql_hbm, kl_hbm, vl_hbm, qs_hbm, ks_hbm, vs_hbm,
    lin_hbm, soft_hbm,
    ql, kl, vl, qs, kt, vv, kown, lin, soft, cumc, cumr, state, mixed, ein, eout, mx, tot, acc, pw,
    in_sem, own_sem, out_sem, kv_recv, dir_send, sib_send, rel_send, ch_send, ch_recv, pw_send, pw_recv,
):
    c = lax.axis_index("ctx")
    z = lax.axis_index("head")
    rows = ql.shape[0]
    chips = n // 2
    chip, core = c // 2, c % 2
    sib = chip * 2 + 1 - core
    group = heads // kvc
    chunks = heads // ch

    start = pl.multiple_of((z * heads // (QUERY_HEADS // KV_HEADS)) * DH, DH)
    own = [
        pltpu.make_async_copy(src.at[:, pl.ds(start, kvc * DH)], dst, own_sem.at[i])
        for i, (src, dst) in enumerate(((ks_hbm, kown), (vs_hbm, vv.at[c])))
    ]
    places = (kt, vv)
    loads = [
        pltpu.make_async_copy(src, dst, in_sem.at[i])
        for i, (src, dst) in enumerate(((kl_hbm, kl), (vl_hbm, vl), (ql_hbm, ql), (qs_hbm, qs)))
    ]
    for copy in own + loads:
        copy.start()

    barrier = pltpu.get_barrier_semaphore()
    for d in range(1, n):
        pl.semaphore_signal(barrier, inc=1, device_id={"ctx": lax.rem(c + d, n)}, device_id_type=MESH)
    for d in range(1, zn):
        pl.semaphore_signal(barrier, inc=1, device_id={"head": lax.rem(z + d, zn)}, device_id_type=MESH)
    pl.semaphore_wait(barrier, n - 1 + zn - 1)

    def kv_copy(block, i, send, target):
        return pltpu.make_async_remote_copy(
            src_ref=places[i].at[block], dst_ref=places[i].at[block],
            send_sem=send, recv_sem=kv_recv.at[block, i],
            device_id={"ctx": target}, device_id_type=MESH,
        )

    def direct(i, to):
        return kv_copy(c, i, dir_send.at[to, i], to * 2 + core)

    def sibling(i):
        return kv_copy(c, i, sib_send.at[i], sib)

    def relayed(i, source):
        return kv_copy(source * 2 + core, i, rel_send.at[source, i], sib)

    def arrived(block, i):
        kv_copy(block, i, sib_send.at[i], sib).wait_recv()

    for copy in own:
        copy.wait()
    kt[c] = kown[...].astype(F32).T.astype(BF16)

    @pl.when(core == 0)
    def _():
        for i in range(2):
            sibling(i).start()

    def send_direct(to, _):
        for i in range(2):
            direct(i, to).start()
        return 0

    near = jnp.minimum(chip + 3, chips)
    lax.fori_loop(chip + 1, near, send_direct, 0)

    def send_far():
        lax.fori_loop(near, chips, send_direct, 0)

    row_id = lax.broadcasted_iota(jnp.int32, (rows, rows), 0)
    col_id = lax.broadcasted_iota(jnp.int32, (rows, rows), 1)
    tri = jnp.where(col_id <= row_id, 1.0, 0.0).astype(F32)
    running = mm(ld_ref[...], tri, 1, 1, HIGHEST)
    cumr[...] = running
    cum = running.T
    for h in range(heads):
        cumc[h] = jnp.broadcast_to(cum[:, h : h + 1], (rows, DH))
    for copy in loads[:2]:
        copy.wait()

    def states(h):
        cc = cumc[h]
        last = cc[rows - 1 : rows, :]
        decayed = (kl[:, cols(h)].astype(F32) * jnp.exp(last - cc)).astype(BF16)
        return [(state, mm(decayed, vl[:, cols(h)], 0, 0))]

    def over_heads(body, count, unroll, base=0):
        unroll = min(unroll, count)

        def step(j, _):
            made = [(base + j * unroll + u, body(base + j * unroll + u)) for u in range(unroll)]
            for h, results in made:
                for ref, value in results:
                    if ref is soft or ref is lin:
                        ref[:, cols(h)] = value
                    else:
                        ref[h] = value
            return 0

        lax.fori_loop(0, count // unroll, step, 0)

    over_heads(states, heads, 4)
    for copy in loads[2:]:
        copy.wait()

    def intra(h):
        q, k, v, cc = ql[:, cols(h)], kl[:, cols(h)], vl[:, cols(h)], cumc[h]
        across = cumr[pl.ds(h, 1), :]
        half = rows // 2
        parts = []
        for low in (0, half):
            high = low + half
            raw = mm(q[low:high], k[:high], 1, 1)
            gap = jnp.concatenate([cc[low:high]] * (high // DH), axis=1) - across[:, :high]
            r = lax.broadcasted_iota(jnp.int32, (half, high), 0) + low
            t = lax.broadcasted_iota(jnp.int32, (half, high), 1)
            w = (raw * jnp.exp(jnp.where(t <= r, gap, NEGATIVE))).astype(BF16)
            parts.append(mm(w, v[:high], 1, 0))
        return [(mixed, jnp.concatenate(parts, axis=0))]

    def chain_copy(j):
        return pltpu.make_async_remote_copy(
            src_ref=eout.at[pl.ds(j * ch, ch)], dst_ref=ein.at[pl.ds(j * ch, ch)],
            send_sem=ch_send.at[j], recv_sem=ch_recv.at[j],
            device_id={"ctx": jnp.minimum(c + 1, n - 1)}, device_id_type=MESH,
        )

    def first_chain():
        def step(j, _):
            part = pl.ds(j * ch, ch)
            eout[part] = state[part].astype(BF16)
            chain_copy(j).start()
            return 0

        lax.fori_loop(0, chunks, step, 0)

    def chain():
        def step(j, _):
            chain_copy(j).wait_recv()

            @pl.when(c < n - 1)
            def _():
                leaving = []
                for u in range(ch):
                    h = j * ch + u
                    fade = jnp.exp(cumc[h, rows - 1 : rows, :])
                    leaving.append((fade * ein[h].astype(F32) + state[h]).astype(BF16))
                for u in range(ch):
                    eout[j * ch + u] = leaving[u]
                chain_copy(j).start()

            return 0

        lax.fori_loop(0, chunks, step, 0)

    def carry():
        def step(j, _):
            made = []
            for u in range(ch):
                h = j * ch + u
                carried = mm(ql[:, cols(h)], ein[h], 1, 0)
                made.append(mixed[h] + carried * jnp.exp(cumc[h]))
            for u in range(ch):
                mixed[j * ch + u] = made[u]
            return 0

        lax.fori_loop(0, chunks, step, 0)

    def power_copy(d):
        return pltpu.make_async_remote_copy(
            src_ref=pw.at[0], dst_ref=pw.at[zn - d],
            send_sem=pw_send.at[d], recv_sem=pw_recv.at[zn - d],
            device_id={"head": lax.rem(z + d, zn)}, device_id_type=MESH,
        )

    def power():
        def step(h, total):
            m = mixed[h]
            return total + m * m

        part = lax.fori_loop(0, heads, step, jnp.zeros((rows, DH), F32))
        pw[0] = mm(jnp.ones((8, DH), F32), part, 1, 1, HIGHEST)
        for d in range(1, zn):
            power_copy(d).start()

    scale = DH ** (-0.5) * LOG2E

    def soft_own():
        for g in range(kvc):
            part = slice(g * DH, (g + 1) * DH)
            keys = kt[c, part, :]
            values = vv[c, :, part]

            def one(h):
                s = mm(qs[:, cols(h)], keys, 1, 0) * scale
                r = lax.broadcasted_iota(jnp.int32, (rows, rows), 0)
                t = lax.broadcasted_iota(jnp.int32, (rows, rows), 1)
                s = jnp.where(t <= r, s, NEGATIVE)
                top = jnp.broadcast_to(jnp.max(s, axis=1, keepdims=True), (rows, DH))
                p = [jnp.exp2(s[:, i : i + DH] - top) for i in range(0, rows, DH)]
                packed = jnp.concatenate([x.astype(BF16) for x in p], axis=1)
                return [(mx, top), (tot, sum(p)), (acc, mm(packed, values, 1, 0))]

            over_heads(one, group, OWN_HEADS, g * group)

    def soft_full(first, count):
        for g in range(kvc):
            part = slice(g * DH, (g + 1) * DH)
            keys = [kt[first + b, part, :] for b in range(count)]
            values = vv[pl.ds(first, count), :, part].reshape(count * rows, DH)

            def one(h):
                q = qs[:, cols(h)]
                s = [mm(q, k, 1, 0) * scale for k in keys]
                before = mx[h]
                high = functools.reduce(jnp.maximum, s)
                top = jnp.maximum(before, jnp.max(high, axis=1, keepdims=True))
                fade = jnp.exp2(before - top)
                p = [jnp.exp2(x[:, i : i + DH] - top) for x in s for i in range(0, rows, DH)]
                packed = jnp.concatenate([x.astype(BF16) for x in p], axis=1)
                return [
                    (mx, top),
                    (tot, tot[h] * fade + sum(p)),
                    (acc, acc[h] * fade + mm(packed, values, 1, 0)),
                ]

            over_heads(one, group, FULL_HEADS, g * group)

    def relay(source):
        for i in range(2):
            arrived(source * 2 + core, i)
            relayed(i, source).start()

    def pair(source):
        for i in range(2):
            arrived(source * 2 + 1 - core, i)
        soft_full(source * 2, 2)

    @pl.when(c == 0)
    def _():
        first_chain()

    @pl.when(c == 1)
    def _():
        chain()

    @pl.when(chip == 0)
    def _():
        send_far()

    over_heads(intra, heads, 4)

    @pl.when(chip > 0)
    def _():
        relay(chip - 1)

    @pl.when(c == 1)
    def _():
        carry()

    @pl.when(chip == 0)
    def _():
        power()

    soft_own()

    @pl.when(core == 1)
    def _():
        for i in range(2):
            arrived(c - 1, i)
        soft_full(c - 1, 1)

    @pl.when(chip > 0)
    def _():
        def step(k, _):
            source = chip - 1 - k

            @pl.when(source == 0)
            def _():
                chain()
                send_far()
                carry()
                power()

            @pl.when(source > 0)
            def _():
                relay(source - 1)

            pair(source)
            return 0

        lax.fori_loop(0, chip, step, 0)

    def soft_end(h):
        return [(soft, (acc[h] / jnp.sum(tot[h], axis=1, keepdims=True)).astype(BF16))]

    over_heads(soft_end, heads, 4)
    soft_out = pltpu.make_async_copy(soft, soft_hbm, out_sem.at[0])
    soft_out.start()

    for d in range(1, zn):
        power_copy(d).wait_recv()
    squares = pw[0]
    for d in range(1, zn):
        squares = squares + pw[d]
    mean = mm(squares, jnp.full((8, DH), 0.125, F32), 0, 0, HIGHEST) / (QUERY_HEADS * DH)
    norm = lax.rsqrt(mean + EPSILON)

    def lin_end(h):
        return [(lin, (mixed[h] * norm * gain_ref[pl.ds(h, 1), :]).astype(BF16))]

    over_heads(lin_end, heads, 4)
    lin_out = pltpu.make_async_copy(lin, lin_hbm, out_sem.at[1])
    lin_out.start()

    for d in range(1, zn):
        power_copy(d).wait_send()

    @pl.when(c < n - 1)
    def _():
        lax.fori_loop(0, chunks, lambda j, _: (chain_copy(j).wait_send(), 0)[1], 0)

    @pl.when(core == 0)
    def _():
        for i in range(2):
            sibling(i).wait_send()

    def sent_direct(to, _):
        for i in range(2):
            direct(i, to).wait_send()
        return 0

    lax.fori_loop(chip + 1, chips, sent_direct, 0)

    def sent_relay(source, _):
        for i in range(2):
            relayed(i, source).wait_send()
        return 0

    lax.fori_loop(0, chip, sent_relay, 0)
    soft_out.wait()
    lin_out.wait()


def local(n, zn, q_linear, k_linear, v_linear, log_decay, norm_gain, q_soft, k_soft, v_soft):
    rows, width = q_linear.shape
    heads = width // DH
    kvc = max(1, heads // (QUERY_HEADS // KV_HEADS))
    ch = 2
    anywhere = pl.BlockSpec(memory_space=pl.ANY)
    whole = pl.BlockSpec(memory_space=pltpu.VMEM)
    dma = pltpu.SemaphoreType.DMA
    chips = n // 2
    chunks = heads // ch
    out = jax.ShapeDtypeStruct((rows, width), BF16)
    wide = pltpu.VMEM((rows, width), BF16)
    per_head = pltpu.VMEM((heads, rows, DH), F32)
    return pl.pallas_call(
        functools.partial(kernel, n, zn, heads, kvc, ch),
        out_shape=(out, out),
        in_specs=[whole, whole] + [anywhere] * 6,
        out_specs=(anywhere, anywhere),
        scratch_shapes=[
            wide, wide, wide, wide,
            pltpu.VMEM((n, kvc * DH, rows), BF16),
            pltpu.VMEM((n, rows, kvc * DH), BF16),
            pltpu.VMEM((rows, kvc * DH), BF16),
            wide, wide,
            per_head,
            pltpu.VMEM((heads, rows), F32),
            pltpu.VMEM((heads, DH, DH), F32),
            per_head,
            pltpu.VMEM((heads, DH, DH), BF16),
            pltpu.VMEM((heads, DH, DH), BF16),
            per_head, per_head, per_head,
            pltpu.VMEM((zn, 8, rows), F32),
            dma((4,)), dma((2,)), dma((2,)),
            dma((n, 2)), dma((chips, 2)), dma((2,)), dma((chips, 2)),
            dma((chunks,)), dma((chunks,)), dma((zn,)), dma((zn,)),
        ],
        compiler_params=pltpu.CompilerParams(
            collective_id=0, has_side_effects=True, vmem_limit_bytes=56 * 2**20
        ),
    )(log_decay.T, norm_gain.reshape(heads, DH), q_linear, k_linear, v_linear, q_soft, k_soft, v_soft)


def solution(mesh):
    n, zn = mesh.shape["ctx"], mesh.shape["head"]
    return jax.shard_map(
        functools.partial(local, n, zn),
        mesh=mesh,
        in_specs=(
            P("ctx", "head"), P("ctx", "head"), P("ctx", "head"), P("ctx", "head"),
            P("head"), P("ctx", "head"), P("ctx", None), P("ctx", None),
        ),
        out_specs=(P("ctx", "head"), P("ctx", "head")),
        check_vma=False,
    )
```

```python
import functools

import jax
import jax.numpy as jnp
from jax import lax
from jax.experimental import pallas as pl
from jax.experimental.pallas import tpu as pltpu
from jax.sharding import PartitionSpec as P

QUERY_HEADS = 64
DH = 128
KV_HEADS = 8
EPSILON = 1e-06
NEGATIVE = -1e30
OWN_HEADS = 8
FULL_HEADS = 8
LOG2E = 1.4426950408889634
MESH = pl.DeviceIdType.MESH
F32 = jnp.float32
BF16 = jnp.bfloat16
HIGHEST = lax.Precision.HIGHEST


def mm(a, b, ca, cb, precision=None):
    return lax.dot_general(
        a, b, (((ca,), (cb,)), ((), ())), preferred_element_type=F32, precision=precision
    )


def cols(index):
    return pl.ds(pl.multiple_of(index * DH, DH), DH)


def kernel(
    n, zn, heads, kvc, ch,
    ld_ref, gain_ref, ql_hbm, kl_hbm, vl_hbm, qs_hbm, ks_hbm, vs_hbm,
    lin_hbm, soft_hbm,
    ql, kl, vl, qs, kt, vv, kown, lin, soft, cumc, cumr, state, mixed, ein, eout, mx, tot, acc, pw,
    in_sem, own_sem, out_sem, kv_recv, dir_send, sib_send, rel_send, ch_send, ch_recv, pw_send, pw_recv,
):
    c = lax.axis_index("ctx")
    z = lax.axis_index("head")
    rows = ql.shape[0]
    chips = n // 2
    chip, core = c // 2, c % 2
    sib = chip * 2 + 1 - core
    group = heads // kvc
    chunks = heads // ch

    start = pl.multiple_of((z * heads // (QUERY_HEADS // KV_HEADS)) * DH, DH)
    own = [
        pltpu.make_async_copy(src.at[:, pl.ds(start, kvc * DH)], dst, own_sem.at[i])
        for i, (src, dst) in enumerate(((ks_hbm, kown), (vs_hbm, vv.at[c])))
    ]
    places = (kt, vv)
    loads = [
        pltpu.make_async_copy(src, dst, in_sem.at[i])
        for i, (src, dst) in enumerate(((kl_hbm, kl), (vl_hbm, vl), (ql_hbm, ql), (qs_hbm, qs)))
    ]
    for copy in own + loads:
        copy.start()

    barrier = pltpu.get_barrier_semaphore()
    for d in range(1, n):
        pl.semaphore_signal(barrier, inc=1, device_id={"ctx": lax.rem(c + d, n)}, device_id_type=MESH)
    for d in range(1, zn):
        pl.semaphore_signal(barrier, inc=1, device_id={"head": lax.rem(z + d, zn)}, device_id_type=MESH)
    pl.semaphore_wait(barrier, n - 1 + zn - 1)

    def kv_copy(block, i, send, target):
        return pltpu.make_async_remote_copy(
            src_ref=places[i].at[block], dst_ref=places[i].at[block],
            send_sem=send, recv_sem=kv_recv.at[block, i],
            device_id={"ctx": target}, device_id_type=MESH,
        )

    def direct(i, to):
        return kv_copy(c, i, dir_send.at[to, i], to * 2 + core)

    def sibling(i):
        return kv_copy(c, i, sib_send.at[i], sib)

    def relayed(i, source):
        return kv_copy(source * 2 + core, i, rel_send.at[source, i], sib)

    def arrived(block, i):
        kv_copy(block, i, sib_send.at[i], sib).wait_recv()

    for copy in own:
        copy.wait()
    kt[c] = kown[...].astype(F32).T.astype(BF16)

    @pl.when(core == 0)
    def _():
        for i in range(2):
            sibling(i).start()

    def send_direct(to, _):
        for i in range(2):
            direct(i, to).start()
        return 0

    lax.fori_loop(chip + 1, chips, send_direct, 0)

    row_id = lax.broadcasted_iota(jnp.int32, (rows, rows), 0)
    col_id = lax.broadcasted_iota(jnp.int32, (rows, rows), 1)
    tri = jnp.where(col_id <= row_id, 1.0, 0.0).astype(F32)
    running = mm(ld_ref[...], tri, 1, 1, HIGHEST)
    cumr[...] = running
    cum = running.T
    for h in range(heads):
        cumc[h] = jnp.broadcast_to(cum[:, h : h + 1], (rows, DH))
    for copy in loads[:2]:
        copy.wait()

    def states(h):
        cc = cumc[h]
        last = cc[rows - 1 : rows, :]
        decayed = (kl[:, cols(h)].astype(F32) * jnp.exp(last - cc)).astype(BF16)
        return [(state, mm(decayed, vl[:, cols(h)], 0, 0))]

    def over_heads(body, count, unroll, base=0):
        unroll = min(unroll, count)

        def step(j, _):
            made = [(base + j * unroll + u, body(base + j * unroll + u)) for u in range(unroll)]
            for h, results in made:
                for ref, value in results:
                    if ref is soft or ref is lin:
                        ref[:, cols(h)] = value
                    else:
                        ref[h] = value
            return 0

        lax.fori_loop(0, count // unroll, step, 0)

    over_heads(states, heads, 4)
    for copy in loads[2:]:
        copy.wait()

    def intra(h):
        q, k, v, cc = ql[:, cols(h)], kl[:, cols(h)], vl[:, cols(h)], cumc[h]
        across = cumr[pl.ds(h, 1), :]
        half = rows // 2
        parts = []
        for low in (0, half):
            high = low + half
            raw = mm(q[low:high], k[:high], 1, 1)
            gap = jnp.concatenate([cc[low:high]] * (high // DH), axis=1) - across[:, :high]
            r = lax.broadcasted_iota(jnp.int32, (half, high), 0) + low
            t = lax.broadcasted_iota(jnp.int32, (half, high), 1)
            w = (raw * jnp.exp(jnp.where(t <= r, gap, NEGATIVE))).astype(BF16)
            parts.append(mm(w, v[:high], 1, 0))
        return [(mixed, jnp.concatenate(parts, axis=0))]

    def chain_copy(j):
        return pltpu.make_async_remote_copy(
            src_ref=eout.at[pl.ds(j * ch, ch)], dst_ref=ein.at[pl.ds(j * ch, ch)],
            send_sem=ch_send.at[j], recv_sem=ch_recv.at[j],
            device_id={"ctx": jnp.minimum(c + 1, n - 1)}, device_id_type=MESH,
        )

    def first_chain():
        def step(j, _):
            part = pl.ds(j * ch, ch)
            eout[part] = state[part].astype(BF16)
            chain_copy(j).start()
            return 0

        lax.fori_loop(0, chunks, step, 0)

    def chain():
        def step(j, _):
            chain_copy(j).wait_recv()

            @pl.when(c < n - 1)
            def _():
                leaving = []
                for u in range(ch):
                    h = j * ch + u
                    fade = jnp.exp(cumc[h, rows - 1 : rows, :])
                    leaving.append((fade * ein[h].astype(F32) + state[h]).astype(BF16))
                for u in range(ch):
                    eout[j * ch + u] = leaving[u]
                chain_copy(j).start()

            return 0

        lax.fori_loop(0, chunks, step, 0)

    def carry():
        def step(j, _):
            made = []
            for u in range(ch):
                h = j * ch + u
                carried = mm(ql[:, cols(h)], ein[h], 1, 0)
                made.append(mixed[h] + carried * jnp.exp(cumc[h]))
            for u in range(ch):
                mixed[j * ch + u] = made[u]
            return 0

        lax.fori_loop(0, chunks, step, 0)

    def power_copy(d):
        return pltpu.make_async_remote_copy(
            src_ref=pw.at[0], dst_ref=pw.at[zn - d],
            send_sem=pw_send.at[d], recv_sem=pw_recv.at[zn - d],
            device_id={"head": lax.rem(z + d, zn)}, device_id_type=MESH,
        )

    def power():
        def step(h, total):
            m = mixed[h]
            return total + m * m

        part = lax.fori_loop(0, heads, step, jnp.zeros((rows, DH), F32))
        pw[0] = mm(jnp.ones((8, DH), F32), part, 1, 1, HIGHEST)
        for d in range(1, zn):
            power_copy(d).start()

    scale = DH ** (-0.5) * LOG2E

    def soft_own():
        for g in range(kvc):
            part = slice(g * DH, (g + 1) * DH)
            keys = kt[c, part, :]
            values = vv[c, :, part]

            def one(h):
                s = mm(qs[:, cols(h)], keys, 1, 0) * scale
                r = lax.broadcasted_iota(jnp.int32, (rows, rows), 0)
                t = lax.broadcasted_iota(jnp.int32, (rows, rows), 1)
                s = jnp.where(t <= r, s, NEGATIVE)
                top = jnp.broadcast_to(jnp.max(s, axis=1, keepdims=True), (rows, DH))
                p = [jnp.exp2(s[:, i : i + DH] - top) for i in range(0, rows, DH)]
                packed = jnp.concatenate([x.astype(BF16) for x in p], axis=1)
                return [(mx, top), (tot, sum(p)), (acc, mm(packed, values, 1, 0))]

            over_heads(one, group, OWN_HEADS, g * group)

    def soft_full(first, count):
        for g in range(kvc):
            part = slice(g * DH, (g + 1) * DH)
            keys = [kt[first + b, part, :] for b in range(count)]
            values = vv[pl.ds(first, count), :, part].reshape(count * rows, DH)

            def one(h):
                q = qs[:, cols(h)]
                s = [mm(q, k, 1, 0) * scale for k in keys]
                before = mx[h]
                high = functools.reduce(jnp.maximum, s)
                top = jnp.maximum(before, jnp.max(high, axis=1, keepdims=True))
                fade = jnp.exp2(before - top)
                p = [jnp.exp2(x[:, i : i + DH] - top) for x in s for i in range(0, rows, DH)]
                packed = jnp.concatenate([x.astype(BF16) for x in p], axis=1)
                return [
                    (mx, top),
                    (tot, tot[h] * fade + sum(p)),
                    (acc, acc[h] * fade + mm(packed, values, 1, 0)),
                ]

            over_heads(one, group, FULL_HEADS, g * group)

    def relay(source):
        for i in range(2):
            arrived(source * 2 + core, i)
            relayed(i, source).start()

    def pair(source):
        for i in range(2):
            arrived(source * 2 + 1 - core, i)
        soft_full(source * 2, 2)

    @pl.when(c == 0)
    def _():
        first_chain()

    @pl.when(c == 1)
    def _():
        chain()

    over_heads(intra, heads, 4)

    @pl.when(chip > 0)
    def _():
        relay(chip - 1)

    @pl.when(c == 1)
    def _():
        carry()

    @pl.when(chip == 0)
    def _():
        power()

    soft_own()

    @pl.when(core == 1)
    def _():
        for i in range(2):
            arrived(c - 1, i)
        soft_full(c - 1, 1)

    @pl.when(chip > 0)
    def _():
        def step(k, _):
            source = chip - 1 - k

            @pl.when(source == 0)
            def _():
                chain()
                carry()
                power()

            @pl.when(source > 0)
            def _():
                relay(source - 1)

            pair(source)
            return 0

        lax.fori_loop(0, chip, step, 0)

    def soft_end(h):
        return [(soft, (acc[h] / jnp.sum(tot[h], axis=1, keepdims=True)).astype(BF16))]

    over_heads(soft_end, heads, 4)
    soft_out = pltpu.make_async_copy(soft, soft_hbm, out_sem.at[0])
    soft_out.start()

    for d in range(1, zn):
        power_copy(d).wait_recv()
    squares = pw[0]
    for d in range(1, zn):
        squares = squares + pw[d]
    mean = mm(squares, jnp.full((8, DH), 0.125, F32), 0, 0, HIGHEST) / (QUERY_HEADS * DH)
    norm = lax.rsqrt(mean + EPSILON)

    def lin_end(h):
        return [(lin, (mixed[h] * norm * gain_ref[pl.ds(h, 1), :]).astype(BF16))]

    over_heads(lin_end, heads, 4)
    lin_out = pltpu.make_async_copy(lin, lin_hbm, out_sem.at[1])
    lin_out.start()

    for d in range(1, zn):
        power_copy(d).wait_send()

    @pl.when(c < n - 1)
    def _():
        lax.fori_loop(0, chunks, lambda j, _: (chain_copy(j).wait_send(), 0)[1], 0)

    @pl.when(core == 0)
    def _():
        for i in range(2):
            sibling(i).wait_send()

    def sent_direct(to, _):
        for i in range(2):
            direct(i, to).wait_send()
        return 0

    lax.fori_loop(chip + 1, chips, sent_direct, 0)

    def sent_relay(source, _):
        for i in range(2):
            relayed(i, source).wait_send()
        return 0

    lax.fori_loop(0, chip, sent_relay, 0)
    soft_out.wait()
    lin_out.wait()


def local(n, zn, q_linear, k_linear, v_linear, log_decay, norm_gain, q_soft, k_soft, v_soft):
    rows, width = q_linear.shape
    heads = width // DH
    kvc = max(1, heads // (QUERY_HEADS // KV_HEADS))
    ch = 2
    anywhere = pl.BlockSpec(memory_space=pl.ANY)
    whole = pl.BlockSpec(memory_space=pltpu.VMEM)
    dma = pltpu.SemaphoreType.DMA
    chips = n // 2
    chunks = heads // ch
    out = jax.ShapeDtypeStruct((rows, width), BF16)
    wide = pltpu.VMEM((rows, width), BF16)
    per_head = pltpu.VMEM((heads, rows, DH), F32)
    return pl.pallas_call(
        functools.partial(kernel, n, zn, heads, kvc, ch),
        out_shape=(out, out),
        in_specs=[whole, whole] + [anywhere] * 6,
        out_specs=(anywhere, anywhere),
        scratch_shapes=[
            wide, wide, wide, wide,
            pltpu.VMEM((n, kvc * DH, rows), BF16),
            pltpu.VMEM((n, rows, kvc * DH), BF16),
            pltpu.VMEM((rows, kvc * DH), BF16),
            wide, wide,
            per_head,
            pltpu.VMEM((heads, rows), F32),
            pltpu.VMEM((heads, DH, DH), F32),
            per_head,
            pltpu.VMEM((heads, DH, DH), BF16),
            pltpu.VMEM((heads, DH, DH), BF16),
            per_head, per_head, per_head,
            pltpu.VMEM((zn, 8, rows), F32),
            dma((4,)), dma((2,)), dma((2,)),
            dma((n, 2)), dma((chips, 2)), dma((2,)), dma((chips, 2)),
            dma((chunks,)), dma((chunks,)), dma((zn,)), dma((zn,)),
        ],
        compiler_params=pltpu.CompilerParams(
            collective_id=0, has_side_effects=True, vmem_limit_bytes=56 * 2**20
        ),
    )(log_decay.T, norm_gain.reshape(heads, DH), q_linear, k_linear, v_linear, q_soft, k_soft, v_soft)


def solution(mesh):
    n, zn = mesh.shape["ctx"], mesh.shape["head"]
    return jax.shard_map(
        functools.partial(local, n, zn),
        mesh=mesh,
        in_specs=(
            P("ctx", "head"), P("ctx", "head"), P("ctx", "head"), P("ctx", "head"),
            P("head"), P("ctx", "head"), P("ctx", None), P("ctx", None),
        ),
        out_specs=(P("ctx", "head"), P("ctx", "head")),
        check_vma=False,
    )
```
